32 devices in a mesh: tensor: 4 (over y, core), adapter: 8 (over z, x).
Axes of the slice: x: 2, y: 2, z: 4, core: 2. Of those that a mesh axis runs over, the one named last changes fastest.
Arguments:
- tokens_in: bfloat16 [128, 8192], P(('tensor', 'adapter')), may hold values from -6 to 6
- w_gate: bfloat16 [8192, 28672], P(None, ('tensor', 'adapter')), may hold values from -0.0625 to 0.0625
- w_up: bfloat16 [8192, 28672], P(None, ('tensor', 'adapter')), may hold values from -0.0625 to 0.0625
- w_down: bfloat16 [28672, 8192], P('tensor', 'adapter'), may hold values from -0.03125 to 0.03125
- a_gate: bfloat16 [8192, 1024], P(None, 'adapter'), may hold values from -0.0625 to 0.0625
- a_up: bfloat16 [8192, 1024], P(None, 'adapter'), may hold values from -0.0625 to 0.0625
- b_gate: bfloat16 [1024, 28672], P(None, ('tensor', 'adapter')), may hold values from -1.5 to 1.5
- b_up: bfloat16 [1024, 28672], P(None, ('tensor', 'adapter')), may hold values from -1.5 to 1.5
- a_down: bfloat16 [28672, 1024], P(('tensor', 'adapter')), may hold values from -0.03125 to 0.03125
- b_down: bfloat16 [1024, 8192], P('adapter'), may hold values from -1.5 to 1.5
- lengths: int32 [8], replicated, may hold values from 1 to 32, 128 in all
- request_adapter: int32 [8], replicated, may hold values from 0 to 63
- placement: int32 [64], replicated, may hold values from 0 to 63, each once
Outputs:
- mixed: bfloat16 [128, 8192], P(('tensor', 'adapter'))
The draws below stay inside these ranges and needn't reach their ends.
Inputs may be any that keep to these rules, and one draw needn't show every extreme that they name: The 8 lengths sum to 128; the longest is exactly 128 // 4. `placement`: each storage slot holds exactly one adapter.
All inputs are finite; a program needn't handle non-finite values.
Results may differ from the reference program's by a relative error of at most 0.0085.
Values may be sent and summed in bfloat16 or wider, within the bound.
A program may use at most 128 MiB of HBM per device.

```python
import math
import jax
import jax.numpy as jnp
import numpy as np

D = 8192
FF = 28672
R = 16
REQS = 8
TOKENS = 128
ADAPTERS = 64


def with_ends(values, stream_key, least, top_value):
    longest = values.shape.index(max(values.shape))
    spots = []
    for shift in (0, 1):
        where = [jax.random.randint(jax.random.fold_in(stream_key, axis), (), 0, length) for axis, length in enumerate(values.shape)]
        where[longest] = (where[longest] + shift) % values.shape[longest]
        spots.append(tuple(where))
    return values.at[spots[0]].set(least).at[spots[1]].set(top_value)


def shard_levels(stream_key, dims, cuts, least, top_value):
    loudness, own = 1.0, jax.random.fold_in(stream_key, 6)
    for axis_at, parts in cuts:
        draws = jnp.exp(jax.random.uniform(jax.random.fold_in(own, axis_at), (parts,), jnp.float32, least / len(cuts), top_value / len(cuts)))
        loudness = loudness * jnp.repeat(draws, dims[axis_at] // parts).reshape([-1 if axis == axis_at else 1 for axis in range(len(dims))])
    return loudness


def length_profile(count, total, most, lean):
    loads = [(1 << 20) // math.isqrt(rank ** lean) + 1 for rank in range(2, count + 1)]
    rest, given = total - most - (count - 1), [1] * (count - 1)
    while rest > 0:
        candidates = [i for i in range(count - 1) if given[i] < most]
        pool, budget = sum([loads[i] for i in candidates]), rest
        for i in candidates:
            extra = min(most - given[i], max(1, budget * loads[i] // pool), rest)
            given[i] = given[i] + extra
            rest = rest - extra
    return np.array([most] + given)


def uneven(key, count, total, bound, lean):
    if count == 2:
        one = jax.random.randint(key, (), max(1, total - bound), min(bound, total - 1) + 1)
        return jnp.stack([one, total - one])
    sizes = jnp.asarray(length_profile(count, total, bound, lean), jnp.int32)
    twos = (count - 1) // 2
    source_of, receiver = sizes[1:1 + 2 * twos:2], sizes[2:2 + 2 * twos:2]
    room = jnp.minimum(source_of - 1, bound - receiver)
    passed = jax.random.randint(jax.random.fold_in(key, 1), (twos,), 0, 1 << 20) % (room + 1)
    sizes = sizes.at[1:1 + 2 * twos:2].set(source_of - passed).at[2:2 + 2 * twos:2].set(receiver + passed)
    return sizes[jax.random.permutation(jax.random.fold_in(key, 2), count)]


def scatter_about(key, extent, deviation, bound, cuts=(), kind=jnp.bfloat16):
    loudness = shard_levels(key, extent, cuts, -0.22, 0.18) if cuts else 1.0
    result = jax.random.normal(key, extent, jnp.float32) * deviation * loudness
    return jnp.minimum(jnp.maximum(result, -bound), bound).astype(kind)


def setup_inputs(seed: int = 0) -> dict:
    arg_keys = jax.random.split(jax.random.key(seed), 14)
    return {
        "tokens_in": scatter_about(arg_keys[0], (TOKENS, D), 1.0, 6.0, ((0, 32),)),
        "w_gate": scatter_about(arg_keys[1], (D, FF), D ** -0.5, 0.0625, ((1, 32),)),
        "w_up": scatter_about(arg_keys[2], (D, FF), D ** -0.5, 0.0625, ((1, 32),)),
        "w_down": scatter_about(arg_keys[3], (FF, D), FF ** -0.5, 0.03125, ((0, 4), (1, 8))),
        "a_gate": scatter_about(arg_keys[4], (D, ADAPTERS * R), D ** -0.5, 0.0625, ((1, 8),)),
        "a_up": scatter_about(arg_keys[5], (D, ADAPTERS * R), D ** -0.5, 0.0625, ((1, 8),)),
        "b_gate": scatter_about(arg_keys[6], (ADAPTERS * R, FF), R ** -0.5, 1.5, ((1, 32),)),
        "b_up": scatter_about(arg_keys[7], (ADAPTERS * R, FF), R ** -0.5, 1.5, ((1, 32),)),
        "a_down": scatter_about(arg_keys[8], (FF, ADAPTERS * R), FF ** -0.5, 0.03125, ((0, 32),)),
        "b_down": scatter_about(arg_keys[9], (ADAPTERS * R, D), R ** -0.5, 1.5, ((0, 8),)),
        "lengths": uneven(arg_keys[10], REQS, TOKENS, TOKENS // 4, 2).astype(jnp.int32),
        "request_adapter": with_ends(jax.random.randint(arg_keys[11], (REQS,), 0, ADAPTERS), jax.random.fold_in(arg_keys[11], 1), 0, ADAPTERS - 1).astype(jnp.int32),
        "placement": jax.random.permutation(arg_keys[12], ADAPTERS).astype(jnp.int32),
    }


def token_tables(lengths, request_adapter, placement, all_tokens):
    positions = jnp.arange(all_tokens, dtype=jnp.int32)
    request_ends = jnp.cumsum(lengths).astype(jnp.int32)
    request = jnp.sum((positions[:, None] >= request_ends[None, :]).astype(jnp.int32), axis=1)
    request_hot = request[:, None] == jnp.arange(lengths.shape[0], dtype=jnp.int32)[None, :]
    adapter = jnp.sum(jnp.where(request_hot, request_adapter[None, :], 0), axis=1).astype(jnp.int32)
    adapter_hot = adapter[:, None] == jnp.arange(placement.shape[0], dtype=jnp.int32)[None, :]
    slot_index = jnp.sum(jnp.where(adapter_hot, placement[None, :], 0), axis=1).astype(jnp.int32)
    return adapter_hot, slot_index


def pick_block(table, hot_rows, rank):
    shaped = table.reshape(table.shape[0], hot_rows.shape[1], rank)
    return jnp.sum(jnp.where(hot_rows[:, :, None], shaped, jnp.zeros_like(shaped)), axis=1)


def spread_block(low_rank, hot_rows):
    spread = jnp.where(hot_rows[:, :, None], low_rank[:, None, :], jnp.zeros_like(low_rank)[:, None, :])
    return spread.reshape(low_rank.shape[0], -1)


def reference(tokens_in, w_gate, w_up, w_down, a_gate, a_up, b_gate, b_up, a_down, b_down, lengths, request_adapter, placement):
    adapter_hot, slot_index = token_tables(lengths, request_adapter, placement, TOKENS)
    slot_hot = slot_index[:, None] == jnp.arange(ADAPTERS, dtype=jnp.int32)[None, :]
    shrunk_gate = pick_block(jnp.dot(tokens_in, a_gate, preferred_element_type=jnp.float32), slot_hot, R).astype(jnp.bfloat16)
    shrunk_up = pick_block(jnp.dot(tokens_in, a_up, preferred_element_type=jnp.float32), slot_hot, R).astype(jnp.bfloat16)
    gate_sum = jnp.dot(tokens_in, w_gate, preferred_element_type=jnp.float32) + jnp.dot(spread_block(shrunk_gate, adapter_hot), b_gate, preferred_element_type=jnp.float32)
    up_sum = jnp.dot(tokens_in, w_up, preferred_element_type=jnp.float32) + jnp.dot(spread_block(shrunk_up, adapter_hot), b_up, preferred_element_type=jnp.float32)
    hidden = (jax.nn.silu(gate_sum) * up_sum).astype(jnp.bfloat16)
    base_sum = jnp.dot(hidden, w_down, preferred_element_type=jnp.float32)
    low_rank = pick_block(jnp.dot(hidden, a_down, preferred_element_type=jnp.float32), adapter_hot, R).astype(jnp.bfloat16)
    delta_down = jnp.dot(spread_block(low_rank, slot_hot), b_down, preferred_element_type=jnp.float32).astype(jnp.bfloat16)
    return (base_sum + delta_down.astype(jnp.float32)).astype(jnp.bfloat16)
```

```python
import functools

import jax
import jax.numpy as jnp
from jax import lax
from jax.experimental import pallas as pl
from jax.experimental.pallas import tpu as pltpu
from jax.sharding import PartitionSpec as P

R = 16
LANES = 128
CHUNKS = 4
MESH = pl.DeviceIdType.MESH
F32 = jnp.float32
BF16 = jnp.bfloat16


def dot(a, b):
    return jnp.dot(a, b, preferred_element_type=F32)


def iota(shape, axis):
    return lax.broadcasted_iota(jnp.int32, shape, axis)


def kernel(
    nt, na, x_ref, wg_ref, wu_ref, wd_ref, ag_ref, au_ref, bg_ref, bu_ref, ad_ref, bd_ref,
    len_ref, radp_ref, plc_ref, out_ref,
    xbuf, xc, perm, wbuf, wd, ab, bgu, ad, bd, acc, acc_s, shr, spread, hbuf, accd,
    breq, br_recv, br_all, low_src, low_recv, low2, bsrc, brecv, packed,
    wsem, lsem, xs_sem, xr_sem, as_sem, ar_sem, ts_sem, tr_sem, hs_sem, hr_sem,
):
    t, a = lax.axis_index("tensor"), lax.axis_index("adapter")
    tokens = acc_s.shape[0]
    f = ad.shape[0]
    d_model = ab.shape[0]
    df = accd.shape[1]
    kc = xc.shape[2]
    kq = d_model // 4
    n = na * nt
    tg = tokens // nt
    rows_t = br_recv.shape[1]
    slots = LANES // R
    reqs = len_ref.shape[0]

    def adapter_copy(src, dst, kind, j, target):
        return pltpu.make_async_remote_copy(
            src_ref=src, dst_ref=dst, send_sem=as_sem.at[kind, j], recv_sem=ar_sem.at[kind, j],
            device_id=(t, target), device_id_type=MESH)

    def tensor_copy(src, dst, kind, j, target):
        return pltpu.make_async_remote_copy(
            src_ref=src, dst_ref=dst, send_sem=ts_sem.at[kind, j], recv_sem=tr_sem.at[kind, j],
            device_id=(target, a), device_id_type=MESH)

    def w_copies(c):
        got = []
        for q in range(4):
            rows = pl.ds(q * kq + c * kc, kc)
            got.append(pltpu.make_async_copy(
                wg_ref.at[rows, :], wbuf.at[c % 2, q, :, pl.ds(0, f)], wsem.at[c % 2, q, 0]))
            got.append(pltpu.make_async_copy(
                wu_ref.at[rows, :], wbuf.at[c % 2, q, :, pl.ds(f, f)], wsem.at[c % 2, q, 1]))
        return got

    x_own = [pltpu.make_async_copy(
        x_ref.at[:, pl.ds(c * kc, kc)], xbuf.at[c, 0], lsem.at[c]) for c in range(CHUNKS)]
    load_bd = pltpu.make_async_copy(bd_ref, bd, lsem.at[4])
    load_ag = pltpu.make_async_copy(ag_ref, ab.at[:, pl.ds(0, LANES)], lsem.at[5])
    load_au = pltpu.make_async_copy(au_ref, ab.at[:, pl.ds(LANES, LANES)], lsem.at[6])
    load_bg = pltpu.make_async_copy(bg_ref, bgu.at[0], lsem.at[7])
    load_bu = pltpu.make_async_copy(bu_ref, bgu.at[1], lsem.at[8])
    load_ad = pltpu.make_async_copy(ad_ref, ad, lsem.at[9])
    load_wd = pltpu.make_async_copy(wd_ref, wd, lsem.at[10])
    for copy in x_own + [load_bd] + w_copies(0) + [load_ag, load_au] + w_copies(1):
        copy.start()
    for copy in (load_bg, load_bu, load_ad, load_wd):
        copy.start()

    barrier = pltpu.get_barrier_semaphore()
    for j in range(1, na):
        pl.semaphore_signal(barrier, inc=1, device_id=(t, (a + j) % na), device_id_type=MESH)
    for j in range(1, nt):
        pl.semaphore_signal(barrier, inc=1, device_id=((t + j) % nt, a), device_id_type=MESH)
    pl.semaphore_wait(barrier, na + nt - 2)

    steps = []
    bit = na // 2
    while bit:
        steps.append((0, bit))
        bit //= 2
    bit = nt // 2
    while bit:
        steps.append((1, bit))
        bit //= 2

    def flip(v, b):
        return v + b - 2 * b * ((v // b) % 2)

    def x_copy(k, c):
        axis, b = steps[k]
        target = (t, flip(a, b)) if axis == 0 else (flip(t, b), a)
        return pltpu.make_async_remote_copy(
            src_ref=xbuf.at[c, pl.ds(0, 1 << k)], dst_ref=xbuf.at[c, pl.ds(1 << k, 1 << k)],
            send_sem=xs_sem.at[k, c], recv_sem=xr_sem.at[k, c],
            device_id=target, device_id_type=MESH)

    last = len(steps) - 1

    def x_start(k, c):
        if k == 0:
            x_own[c].wait()
        else:
            x_copy(k - 1, c).wait_recv()
        x_copy(k, c).start()

    for wave in range(CHUNKS + last - 1):
        for k in range(last):
            if 0 <= wave - k < CHUNKS:
                x_start(k, wave - k)

    def tables(rows, first):
        position = iota((rows, LANES), 0) + first
        adapter = jnp.zeros((rows, LANES), jnp.int32)
        slot = jnp.zeros((rows, LANES), jnp.int32)
        request = jnp.zeros((rows, LANES), jnp.int32)
        start = 0
        for r in range(reqs):
            end = start + len_ref[r]
            inside = (position >= start) & (position < end)
            adapter = jnp.where(inside, radp_ref[r], adapter)
            slot = jnp.where(inside, plc_ref[radp_ref[r]], slot)
            request = jnp.where(inside, r, request)
            start = end
        return adapter, slot, request

    row, col = iota((LANES, LANES), 0), iota((LANES, LANES), 1)
    slot_of_row = jnp.full((LANES, LANES), -1, jnp.int32)
    for r in range(reqs):
        slot_of_row = jnp.where(row // R == r, plc_ref[radp_ref[r]], slot_of_row)
    choose = (slot_of_row == a * slots + col // R) & (row % R == col % R)
    choose = jnp.where(choose, 1.0, 0.0).astype(BF16)
    load_bd.wait()

    def choose_block(i, carry):
        off = pl.multiple_of(i * df, LANES)
        breq[i] = dot(choose, bd[:, pl.ds(off, df)]).astype(BF16)
        return carry

    lax.fori_loop(0, na, choose_block, 0)
    own_rows = pl.ds(pl.multiple_of(t * rows_t, rows_t), rows_t)

    def br_copy(j):
        target = (a + j) % na
        return adapter_copy(breq.at[target, own_rows], br_recv.at[j], 0, j, target)

    for j in range(1, na):
        br_copy(j).start()
    br_recv[0] = breq[a, own_rows]

    def perm_block(q, carry):
        p_row, p_col = iota((tokens, n * 16), 0), iota((tokens, n * 16), 1)
        s, i, pq = p_col // 16, (p_col % 16) // 4, p_col % 4
        src_t, src_a = jnp.full_like(s, t), jnp.full_like(s, a)
        for k, (axis, b) in enumerate(steps):
            on = ((s // (1 << k)) % 2) == 1
            if axis == 0:
                src_a = jnp.where(on, src_a + (b - 2 * b * ((a // b) % 2)), src_a)
            else:
                src_t = jnp.where(on, src_t + (b - 2 * b * ((t // b) % 2)), src_t)
        hit = (p_row == (src_t * na + src_a) * 4 + i) & (pq == q)
        perm[q] = jnp.where(hit, 1.0, 0.0).astype(BF16)
        return carry

    lax.fori_loop(0, 4, perm_block, 0)
    adapter_t, slot_t, _ = tables(tokens, 0)

    tile = 256 if (2 * f) % 256 == 0 else LANES
    x_start(last, 0)
    for c in range(CHUNKS):
        if c + 1 < CHUNKS:
            x_start(last, c + 1)
        x_copy(last, c).wait_recv()

        def arrange(q, carry):
            block = xbuf[c].reshape(n * 16, kc)
            xc[q] = dot(perm[q], block).astype(BF16)
            return carry

        lax.fori_loop(0, 4, arrange, 0)
        if c == 0:
            load_ag.wait()
            load_au.wait()
        part = dot(xc[0], ab[pl.ds(c * kc, kc), :])
        for q in range(1, 4):
            part += dot(xc[q], ab[pl.ds(q * kq + c * kc, kc), :])
        if c == 0:
            acc_s[...] = part
        else:
            acc_s[...] += part

        if c == CHUNKS - 1:
            total = jnp.zeros((tokens // 4, LANES), F32)
            for h in range(2):
                kept = jnp.where(slot_t == a * slots + iota((tokens, LANES), 1) // R,
                                 acc_s[:, h * LANES:(h + 1) * LANES], 0.0).astype(BF16)
                for g in range(4):
                    to = (col // 32 == g) & ((col % 32) // R == h) & (row % R == col % R)
                    total += dot(kept[g * (tokens // 4):(g + 1) * (tokens // 4)],
                                 jnp.where(to, 1.0, 0.0).astype(BF16))
            shr[0] = total.astype(BF16)
            for j in range(1, na):
                adapter_copy(shr.at[0], shr.at[j], 1, j, (a + j) % na).start()

        for copy in w_copies(c):
            copy.wait()

        def gate_up(i, carry):
            cols = pl.ds(pl.multiple_of(i * tile, tile), tile)
            s = dot(xc[0], wbuf[c % 2, 0, :, cols])
            for q in range(1, 4):
                s += dot(xc[q], wbuf[c % 2, q, :, cols])
            if c == 0:
                acc[:, cols] = s
            else:
                acc[:, cols] += s
            return carry

        lax.fori_loop(0, 2 * f // tile, gate_up, 0)
        if c + 2 < CHUNKS:
            for copy in w_copies(c + 2):
                copy.start()

    for j in range(1, na):
        br_copy(j).wait_recv()
    rows_sum = br_recv[0].astype(F32)
    for j in range(1, na):
        rows_sum += br_recv[j].astype(F32)
    br_all[t] = rows_sum.astype(BF16)
    for j in range(1, nt):
        tensor_copy(br_all.at[t], br_all.at[t], 0, j, (t + j) % nt).start()

    for j in range(1, na):
        adapter_copy(shr.at[0], shr.at[j], 1, j, (a + j) % na).wait_recv()
    shrunk = shr[0].astype(F32)
    for j in range(1, na):
        shrunk += shr[j].astype(F32)
    shrunk = shrunk.astype(BF16)
    load_bg.wait()
    load_bu.wait()
    quarter = tokens // 4
    for h in range(2):
        for g in range(4):
            frm = (row // 32 == g) & ((row % 32) // R == h) & (row % R == col % R)
            value = dot(shrunk, jnp.where(frm, 1.0, 0.0).astype(BF16))
            ids = adapter_t[g * quarter:(g + 1) * quarter]
            lane = iota((quarter, LANES), 1) // R
            for blk in range(spread.shape[2] // LANES):
                spread[h, g * quarter:(g + 1) * quarter, blk * LANES:(blk + 1) * LANES] = jnp.where(
                    ids == blk * slots + lane, value, 0.0).astype(BF16)

    def make_hidden(i, carry):
        cols = pl.ds(pl.multiple_of(i * LANES, LANES), LANES)
        up_cols = pl.ds(pl.multiple_of(f + i * LANES, LANES), LANES)
        gate = acc[:, cols] + dot(spread[0], bgu[0, :, cols])
        up = acc[:, up_cols] + dot(spread[1], bgu[1, :, cols])
        hbuf[0, :, cols] = (gate / (1.0 + jnp.exp(-gate)) * up).astype(BF16)
        return carry

    lax.fori_loop(0, f // LANES, make_hidden, 0)

    half = na // 2
    mate = flip(a, 1)

    def h_copy(j):
        if j < half:
            src, dst, target = hbuf.at[0], hbuf.at[j], (a + 2 * j) % na
        else:
            src, dst, target = hbuf.at[j - half], hbuf.at[j], mate
        return pltpu.make_async_remote_copy(
            src_ref=src, dst_ref=dst, send_sem=hs_sem.at[j], recv_sem=hr_sem.at[j],
            device_id=(t, target), device_id_type=MESH)

    h_copy(half).start()
    for j in range(1, half):
        h_copy(j).start()

    load_ad.wait()

    def low_block(i, carry):
        cols = pl.ds(pl.multiple_of(i * LANES, LANES), LANES)
        value = dot(hbuf[0], ad[:, cols])
        return carry + jnp.where(adapter_t == i * slots + iota((tokens, LANES), 1) // R, value, 0.0)

    low = lax.fori_loop(0, ad.shape[1] // LANES, low_block, jnp.zeros((tokens, LANES), F32))
    same = jnp.where(row % R == col % R, 1.0, 0.0).astype(BF16)
    low = dot(low.astype(BF16), same).astype(BF16)
    for g in range(nt):
        low_src[g] = low[g * tg:(g + 1) * tg]

    def low_copy(j):
        return tensor_copy(low_src.at[(t + j) % nt], low_recv.at[j], 1, j, (t + j) % nt)

    for j in range(1, nt):
        low_copy(j).start()
    low_recv[0] = low_src[t]
    for j in range(1, nt):
        low_copy(j).wait_recv()
    low_sum = low_recv[0].astype(F32)
    for j in range(1, nt):
        low_sum += low_recv[j].astype(F32)
    low2[0] = low_sum.astype(BF16)
    for j in range(1, na):
        adapter_copy(low2.at[0], low2.at[j], 2, j, (a + j) % na).start()

    load_wd.wait()

    dtile = 256 if df % 256 == 0 else LANES

    def down(j, source, first):
        def body(i, carry):
            cols = pl.ds(pl.multiple_of(i * dtile, dtile), dtile)
            value = dot(hbuf[j], wd[source, :, cols])
            if first:
                accd[:, cols] = value
            else:
                accd[:, cols] += value
            return carry

        lax.fori_loop(0, df // dtile, body, 0)

    down(0, a, True)
    for j in range(1, half):
        h_copy(j).wait_recv()
        h_copy(half + j).start()
        down(j, (a + na - 2 * j) % na, False)
    for j in range(half):
        h_copy(half + j).wait_recv()
        down(half + j, (mate + na - 2 * j) % na, False)

    for g in range(nt):
        bsrc[g] = accd[g * tg:(g + 1) * tg].astype(BF16)

    def base_copy(j):
        return tensor_copy(bsrc.at[(t + j) % nt], brecv.at[j], 2, j, (t + j) % nt)

    for j in range(1, nt):
        base_copy(j).start()
    brecv[0] = bsrc[t]

    for j in range(1, na):
        adapter_copy(low2.at[0], low2.at[j], 2, j, (a + j) % na).wait_recv()
    low_all = low2[0].astype(F32)
    for j in range(1, na):
        low_all += low2[j].astype(F32)
    _, _, request_g = tables(tg, t * tg)
    low_all = jnp.where(request_g == iota((tg, LANES), 1) // R, low_all, 0.0).astype(BF16)
    for j in range(1, nt):
        other = (t + nt - j) % nt
        tensor_copy(br_all.at[other], br_all.at[other], 0, j, (t + j) % nt).wait_recv()
    delta = dot(low_all, br_all[...].reshape(nt * rows_t, df)).astype(BF16).astype(F32)

    for j in range(1, nt):
        base_copy(j).wait_recv()
    base = brecv[0].astype(F32)
    for j in range(1, nt):
        base += brecv[j].astype(F32)
    mixed = (base + delta).astype(BF16)

    fq = df // 4
    o_row, o_col = iota((na * 16, tg), 0), iota((na * 16, tg), 1)
    result = jnp.zeros((na * 16, fq), F32)
    for q in range(4):
        hit = ((o_row % 16) // 4 == q) & (o_col == (o_row // 16) * 4 + o_row % 4)
        result += dot(jnp.where(hit, 1.0, 0.0).astype(BF16), mixed[:, q * fq:(q + 1) * fq])
    packed[...] = result.astype(BF16).reshape(na, 16, fq)

    def out_copy(j):
        target = (a + j) % na
        return adapter_copy(packed.at[target], out_ref.at[a], 3, j, target)

    for j in range(1, na):
        out_copy(j).start()
    out_ref[a] = packed[a]
    for j in range(1, na):
        other = (a + na - j) % na
        adapter_copy(packed.at[other], out_ref.at[other], 3, j, other).wait_recv()

    for k in range(len(steps)):
        for c in range(CHUNKS):
            x_copy(k, c).wait_send()
    for j in range(1, na):
        br_copy(j).wait_send()
        adapter_copy(shr.at[0], shr.at[j], 1, j, (a + j) % na).wait_send()
        adapter_copy(low2.at[0], low2.at[j], 2, j, (a + j) % na).wait_send()
        out_copy(j).wait_send()
        h_copy(j).wait_send()
    for j in range(1, nt):
        tensor_copy(br_all.at[t], br_all.at[t], 0, j, (t + j) % nt).wait_send()
        low_copy(j).wait_send()
        base_copy(j).wait_send()


def local(nt, na, x, w_gate, w_up, w_down, a_gate, a_up, b_gate, b_up, a_down, b_down,
          lengths, request_adapter, placement):
    tok, d_model = x.shape
    tokens = tok * nt * na
    f0 = w_gate.shape[1]
    f = -(-f0 // LANES) * LANES
    df = w_down.shape[1]
    w_down = w_down.reshape(na, f0, df)
    if f != f0:
        wide = ((0, 0), (0, f - f0))
        w_gate, w_up = jnp.pad(w_gate, wide), jnp.pad(w_up, wide)
        b_gate, b_up = jnp.pad(b_gate, wide), jnp.pad(b_up, wide)
        a_down = jnp.pad(a_down, ((0, f - f0), (0, 0)))
        w_down = jnp.pad(w_down, ((0, 0), (0, f - f0), (0, 0)))
    x = x.reshape(tok * 4, d_model // 4)
    n = nt * na
    kc = d_model // 4 // CHUNKS
    ranks = b_gate.shape[0]
    rows_t = LANES // nt
    tg = tokens // nt
    nsteps = n.bit_length() - 1
    anyspace = pl.BlockSpec(memory_space=pl.ANY)
    smem = pl.BlockSpec(memory_space=pltpu.SMEM)
    dma = pltpu.SemaphoreType.DMA
    out = pl.pallas_call(
        functools.partial(kernel, nt, na),
        out_shape=jax.ShapeDtypeStruct((na, 16, df // 4), BF16),
        in_specs=[anyspace] * 10 + [smem] * 3,
        out_specs=pl.BlockSpec(memory_space=pltpu.VMEM),
        scratch_shapes=[
            pltpu.VMEM((CHUNKS, n, 16, kc), BF16),
            pltpu.VMEM((4, tokens, kc), BF16),
            pltpu.VMEM((4, tokens, n * 16), BF16),
            pltpu.VMEM((2, 4, kc, 2 * f), BF16),
            pltpu.VMEM((na, f, df), BF16),
            pltpu.VMEM((d_model, 2 * LANES), BF16),
            pltpu.VMEM((2, ranks, f), BF16),
            pltpu.VMEM((f, ranks), BF16),
            pltpu.VMEM((LANES, b_down.shape[1]), BF16),
            pltpu.VMEM((tokens, 2 * f), F32),
            pltpu.VMEM((tokens, 2 * LANES), F32),
            pltpu.VMEM((na, tokens // 4, LANES), BF16),
            pltpu.VMEM((2, tokens, ranks), BF16),
            pltpu.VMEM((na, tokens, f), BF16),
            pltpu.VMEM((tokens, df), F32),
            pltpu.VMEM((na, LANES, df), BF16),
            pltpu.VMEM((na, rows_t, df), BF16),
            pltpu.VMEM((nt, rows_t, df), BF16),
            pltpu.VMEM((nt, tg, LANES), BF16),
            pltpu.VMEM((nt, tg, LANES), BF16),
            pltpu.VMEM((na, tg, LANES), BF16),
            pltpu.VMEM((nt, tg, df), BF16),
            pltpu.VMEM((nt, tg, df), BF16),
            pltpu.VMEM((na, 16, df // 4), BF16),
            dma((2, 4, 2)),
            dma((11,)),
            dma((nsteps, CHUNKS)),
            dma((nsteps, CHUNKS)),
            dma((4, na)),
            dma((4, na)),
            dma((3, nt)),
            dma((3, nt)),
            dma((na,)),
            dma((na,)),
        ],
        compiler_params=pltpu.CompilerParams(
            collective_id=0, has_side_effects=True, vmem_limit_bytes=60 * 1024 * 1024),
    )(x, w_gate, w_up, w_down, a_gate, a_up, b_gate, b_up, a_down, b_down,
      lengths, request_adapter, placement)
    out = out.reshape(na, 4, tok, df // 4).transpose(2, 0, 1, 3)
    return out.reshape(tok, na * df)


def solution(mesh):
    nt, na = mesh.shape["tensor"], mesh.shape["adapter"]
    both = ("tensor", "adapter")
    in_specs = (
        P(both, None),
        P(None, both),
        P(None, both),
        P("tensor", "adapter"),
        P(None, "adapter"),
        P(None, "adapter"),
        P(None, both),
        P(None, both),
        P(both, None),
        P("adapter", None),
        P(),
        P(),
        P(),
    )
    return jax.shard_map(
        functools.partial(local, nt, na), mesh=mesh, in_specs=in_specs,
        out_specs=P(both, None), check_vma=False)
```

```python
import functools

import jax
import jax.numpy as jnp
from jax import lax
from jax.experimental import pallas as pl
from jax.experimental.pallas import tpu as pltpu
from jax.sharding import PartitionSpec as P

R = 16
LANES = 128
CHUNKS = 4
MESH = pl.DeviceIdType.MESH
F32 = jnp.float32
BF16 = jnp.bfloat16


def dot(a, b):
    return jnp.dot(a, b, preferred_element_type=F32)


def iota(shape, axis):
    return lax.broadcasted_iota(jnp.int32, shape, axis)


def kernel(
    nt, na, pieces, x_ref, wg_ref, wu_ref, wd_ref, ag_ref, au_ref, bg_ref, bu_ref, ad_ref, bd_ref,
    len_ref, radp_ref, plc_ref, out_ref,
    xbuf, xc, split, canon, wbuf, wd, ab, bgu, bsel, ad, bd, acc, acc_s, shr, spread, hbuf, accd,
    breq, br_recv, br_all, low_src, low_recv, low2, bsrc, brecv, packed,
    wsem, lsem, xs_sem, xr_sem, as_sem, ar_sem, ts_sem, tr_sem, hs_sem, hr_sem,
):
    t, a = lax.axis_index("tensor"), lax.axis_index("adapter")
    tokens = acc_s.shape[0]
    f = ad.shape[0]
    d_model = ab.shape[0]
    df = accd.shape[1]
    kc = xc.shape[3]
    kq = d_model // 4
    n = na * nt
    tg = tokens // nt
    rows_t = br_recv.shape[1]
    slots = LANES // R
    reqs = len_ref.shape[0]

    def adapter_copy(src, dst, kind, j, target):
        return pltpu.make_async_remote_copy(
            src_ref=src, dst_ref=dst, send_sem=as_sem.at[kind, j], recv_sem=ar_sem.at[kind, j],
            device_id=(t, target), device_id_type=MESH)

    def tensor_copy(src, dst, kind, j, target):
        return pltpu.make_async_remote_copy(
            src_ref=src, dst_ref=dst, send_sem=ts_sem.at[kind, j], recv_sem=tr_sem.at[kind, j],
            device_id=(target, a), device_id_type=MESH)

    def w_copies(c):
        got = []
        for q in range(4):
            rows = pl.ds(q * kq + c * kc, kc)
            got.append(pltpu.make_async_copy(
                wg_ref.at[rows, :], wbuf.at[c % 2, q, :, pl.ds(0, f)], wsem.at[c % 2, q, 0]))
            got.append(pltpu.make_async_copy(
                wu_ref.at[rows, :], wbuf.at[c % 2, q, :, pl.ds(f, f)], wsem.at[c % 2, q, 1]))
        return got

    x_own = [pltpu.make_async_copy(
        x_ref.at[:, pl.ds(c * kc, kc)], xbuf.at[c, 0], lsem.at[c]) for c in range(CHUNKS)]
    load_bd = pltpu.make_async_copy(bd_ref, bd, lsem.at[4])
    load_ag = pltpu.make_async_copy(ag_ref, ab.at[:, pl.ds(0, LANES)], lsem.at[5])
    load_au = pltpu.make_async_copy(au_ref, ab.at[:, pl.ds(LANES, LANES)], lsem.at[6])
    load_bg = pltpu.make_async_copy(bg_ref, bgu.at[0], lsem.at[7])
    load_bu = pltpu.make_async_copy(bu_ref, bgu.at[1], lsem.at[8])
    load_ad = pltpu.make_async_copy(ad_ref, ad, lsem.at[9])
    load_wd = pltpu.make_async_copy(wd_ref, wd, lsem.at[10])
    for copy in x_own + [load_bd] + w_copies(0) + [load_ag, load_au] + w_copies(1):
        copy.start()
    for copy in (load_bg, load_bu, load_ad, load_wd):
        copy.start()

    barrier = pltpu.get_barrier_semaphore()
    for j in range(1, na):
        pl.semaphore_signal(barrier, inc=1, device_id=(t, (a + j) % na), device_id_type=MESH)
    for j in range(1, nt):
        pl.semaphore_signal(barrier, inc=1, device_id=((t + j) % nt, a), device_id_type=MESH)
    pl.semaphore_wait(barrier, na + nt - 2)

    steps = []
    bit = na // 2
    while bit:
        steps.append((0, bit))
        bit //= 2
    bit = nt // 2
    while bit:
        steps.append((1, bit))
        bit //= 2

    def flip(v, b):
        return v + b - 2 * b * ((v // b) % 2)

    def x_copy(k, c):
        axis, b = steps[k]
        target = (t, flip(a, b)) if axis == 0 else (flip(t, b), a)
        return pltpu.make_async_remote_copy(
            src_ref=xbuf.at[c, pl.ds(0, 1 << k)], dst_ref=xbuf.at[c, pl.ds(1 << k, 1 << k)],
            send_sem=xs_sem.at[k, c], recv_sem=xr_sem.at[k, c],
            device_id=target, device_id_type=MESH)

    last = len(steps) - 1

    def x_start(k, c):
        if k == 0:
            x_own[c].wait()
        else:
            x_copy(k - 1, c).wait_recv()
        x_copy(k, c).start()

    for wave in range(CHUNKS + last - 1):
        for k in range(last):
            if 0 <= wave - k < CHUNKS:
                x_start(k, wave - k)

    def tables(rows, first):
        position = iota((rows, LANES), 0) + first
        adapter = jnp.zeros((rows, LANES), jnp.int32)
        slot = jnp.zeros((rows, LANES), jnp.int32)
        request = jnp.zeros((rows, LANES), jnp.int32)
        start = 0
        for r in range(reqs):
            end = start + len_ref[r]
            inside = (position >= start) & (position < end)
            adapter = jnp.where(inside, radp_ref[r], adapter)
            slot = jnp.where(inside, plc_ref[radp_ref[r]], slot)
            request = jnp.where(inside, r, request)
            start = end
        return adapter, slot, request

    row, col = iota((LANES, LANES), 0), iota((LANES, LANES), 1)
    slot_of_row = jnp.full((LANES, LANES), -1, jnp.int32)
    for r in range(reqs):
        slot_of_row = jnp.where(row // R == r, plc_ref[radp_ref[r]], slot_of_row)
    choose = (slot_of_row == a * slots + col // R) & (row % R == col % R)
    choose = jnp.where(choose, 1.0, 0.0).astype(BF16)
    load_bd.wait()

    def choose_block(i, carry):
        off = pl.multiple_of(i * df, LANES)
        breq[i] = dot(choose, bd[:, pl.ds(off, df)]).astype(BF16)
        return carry

    lax.fori_loop(0, na, choose_block, 0)
    own_rows = pl.ds(pl.multiple_of(t * rows_t, rows_t), rows_t)

    def br_copy(j):
        target = (a + j) % na
        return adapter_copy(breq.at[target, own_rows], br_recv.at[j], 0, j, target)

    for j in range(1, na):
        br_copy(j).start()
    br_recv[0] = breq[a, own_rows]

    s_row, s_col = iota((256, 256), 0), iota((256, 256), 1)
    hit = (s_row // 64 == s_col % 4) & (s_row % 64 == s_col // 4)
    split[...] = jnp.where(hit, 1.0, 0.0).astype(BF16)

    def owner_row(place):
        s = place // 4
        src_t, src_a = jnp.full_like(s, t), jnp.full_like(s, a)
        for k, (axis, b) in enumerate(steps):
            on = ((s // (1 << k)) % 2) == 1
            if axis == 0:
                src_a = jnp.where(on, src_a + (b - 2 * b * ((a // b) % 2)), src_a)
            else:
                src_t = jnp.where(on, src_t + (b - 2 * b * ((t // b) % 2)), src_t)
        return (src_t * na + src_a) * 4 + place % 4

    c_row, c_col = iota((tokens, tokens), 0), iota((tokens, tokens), 1)
    canon[0] = jnp.where(c_row == owner_row(c_col), 1.0, 0.0).astype(BF16)
    canon[1] = jnp.where(c_col == owner_row(c_row), 1.0, 0.0).astype(BF16)
    adapter_t, slot_t, request_t = tables(tokens, 0)

    tile = 256
    quarter = tokens // 4

    def arrive(c):
        if c + 1 < CHUNKS:
            x_start(last, c + 1)
        x_copy(last, c).wait_recv()

        def arrange(g, carry):
            block = xbuf[c, pl.ds(g * 16, 16)].reshape(256, kc)
            value = dot(split[...], block).astype(BF16)
            for q in range(4):
                xc[c % 2, q, pl.ds(pl.multiple_of(g * 64, 64), 64)] = value[q * 64:(q + 1) * 64]
            return carry

        lax.fori_loop(0, n // 16, arrange, 0)
        if c == 0:
            load_ag.wait()
            load_au.wait()
        part = dot(xc[c % 2, 0], ab[pl.ds(c * kc, kc), :])
        for q in range(1, 4):
            part += dot(xc[c % 2, q], ab[pl.ds(q * kq + c * kc, kc), :])
        if c == 0:
            acc_s[...] = part
        else:
            acc_s[...] += part

    def gate_up(c, i):
        cols = pl.ds(pl.multiple_of(i * tile, tile), tile)
        s = dot(xc[c % 2, 0], wbuf[c % 2, 0, :, cols])
        for q in range(1, 4):
            s += dot(xc[c % 2, q], wbuf[c % 2, q, :, cols])
        if c == 0:
            acc[:, cols] = s
        else:
            acc[:, cols] += s

    def whole_chunk(c):
        for copy in w_copies(c):
            copy.wait()

        def body(i, carry):
            gate_up(c, i)
            return carry

        lax.fori_loop(0, 2 * f // tile, body, 0)
        if c + 2 < CHUNKS:
            for copy in w_copies(c + 2):
                copy.start()

    x_start(last, 0)
    for c in range(CHUNKS - 2):
        arrive(c)
        whole_chunk(c)
    arrive(CHUNKS - 2)
    arrive(CHUNKS - 1)

    ordered = dot(canon[0], acc_s[...].astype(BF16))
    total = jnp.zeros((quarter, LANES), F32)
    for h in range(2):
        kept = jnp.where(slot_t == a * slots + iota((tokens, LANES), 1) // R,
                         ordered[:, h * LANES:(h + 1) * LANES], 0.0).astype(BF16)
        for g in range(4):
            to = (col // 32 == g) & ((col % 32) // R == h) & (row % R == col % R)
            total += dot(kept[g * quarter:(g + 1) * quarter],
                         jnp.where(to, 1.0, 0.0).astype(BF16))
    shr[0] = total.astype(BF16)
    for j in range(1, na):
        adapter_copy(shr.at[0], shr.at[j], 1, j, (a + j) % na).start()

    whole_chunk(CHUNKS - 2)

    load_bg.wait()
    load_bu.wait()
    for r in range(reqs):
        for h in range(2):
            bsel[h, r * R:(r + 1) * R] = bgu[h, radp_ref[r]]
    for j in range(1, na):
        adapter_copy(shr.at[0], shr.at[j], 1, j, (a + j) % na).wait_recv()
    shrunk = shr[0].astype(F32)
    for j in range(1, na):
        shrunk += shr[j].astype(F32)
    shrunk = shrunk.astype(BF16)
    for h in range(2):
        parts = []
        for g in range(4):
            frm = (row // 32 == g) & ((row % 32) // R == h) & (row % R == col % R)
            parts.append(dot(shrunk, jnp.where(frm, 1.0, 0.0).astype(BF16)))
        value = jnp.concatenate(parts, axis=0)
        value = jnp.where(request_t == iota((tokens, LANES), 1) // R, value, 0.0).astype(BF16)
        spread[h] = dot(canon[1], value).astype(BF16)

    half = na // 2
    mate = flip(a, 1)

    def h_copy(p, j):
        cols = pl.ds(pieces[p][0], pieces[p][1] - pieces[p][0])
        frm = 0 if j < half else j - half
        target = (a + 2 * j) % na if j < half else mate
        return pltpu.make_async_remote_copy(
            src_ref=hbuf.at[frm, :, cols], dst_ref=hbuf.at[j, :, cols],
            send_sem=hs_sem.at[p, j], recv_sem=hr_sem.at[p, j],
            device_id=(t, target), device_id_type=MESH)

    for copy in w_copies(CHUNKS - 1):
        copy.wait()
    full, odd = f // 256, (f // LANES) % 2
    for p, (lo, hi) in enumerate(pieces):
        tiles = [p] if p < full else []
        if odd and p == 0:
            tiles.append(full)
        if p < full:
            tiles.append(full + odd + p)
        for i in tiles:
            gate_up(CHUNKS - 1, i)
        for c0 in range(lo, hi, LANES):
            gate = acc[:, c0:c0 + LANES] + dot(spread[0], bsel[0, :, c0:c0 + LANES])
            up = acc[:, f + c0:f + c0 + LANES] + dot(spread[1], bsel[1, :, c0:c0 + LANES])
            value = (gate / (1.0 + jnp.exp(-gate)) * up).astype(BF16)
            hbuf[0, :, c0:c0 + LANES] = dot(canon[0], value).astype(BF16)
        h_copy(p, half).start()
        for j in range(1, half):
            h_copy(p, j).start()

    for j in range(1, na):
        br_copy(j).wait_recv()
    rows_sum = br_recv[0].astype(F32)
    for j in range(1, na):
        rows_sum += br_recv[j].astype(F32)
    br_all[t] = rows_sum.astype(BF16)
    for j in range(1, nt):
        tensor_copy(br_all.at[t], br_all.at[t], 0, j, (t + j) % nt).start()

    load_ad.wait()

    def low_block(i, carry):
        cols = pl.ds(pl.multiple_of(i * 256, 256), 256)
        value = dot(hbuf[0], ad[:, cols])
        for h in range(2):
            owner = (2 * i + h) * slots + iota((tokens, LANES), 1) // R
            carry += jnp.where(adapter_t == owner, value[:, h * LANES:(h + 1) * LANES], 0.0)
        return carry

    low = lax.fori_loop(0, ad.shape[1] // 256, low_block, jnp.zeros((tokens, LANES), F32))
    same = jnp.where(row % R == col % R, 1.0, 0.0).astype(BF16)
    low = dot(low.astype(BF16), same).astype(BF16)
    for g in range(nt):
        low_src[g] = low[g * tg:(g + 1) * tg]

    def low_copy(j):
        return tensor_copy(low_src.at[(t + j) % nt], low_recv.at[j], 1, j, (t + j) % nt)

    for j in range(1, nt):
        low_copy(j).start()
    low_recv[0] = low_src[t]
    for j in range(1, nt):
        low_copy(j).wait_recv()
    low_sum = low_recv[0].astype(F32)
    for j in range(1, nt):
        low_sum += low_recv[j].astype(F32)
    low2[0] = low_sum.astype(BF16)
    for j in range(1, na):
        adapter_copy(low2.at[0], low2.at[j], 2, j, (a + j) % na).start()

    load_wd.wait()

    dtile = 256 if df % 256 == 0 else LANES

    def down(p, j, source, first=False):
        lo, hi = pieces[p]

        def body(i, carry):
            cols = pl.ds(pl.multiple_of(i * dtile, dtile), dtile)
            value = dot(hbuf[j, :, lo:hi], wd[source, lo:hi, cols])
            if first:
                accd[:, cols] = value
            else:
                accd[:, cols] += value
            return carry

        lax.fori_loop(0, df // dtile, body, 0)

    for p in range(len(pieces)):
        for j in range(1, half):
            h_copy(p, j).wait_recv()
            h_copy(p, half + j).start()
        down(p, 0, a, p == 0)
        for j in range(1, half):
            down(p, j, (a + na - 2 * j) % na)
    for p in range(len(pieces)):
        for j in range(half):
            h_copy(p, half + j).wait_recv()
            down(p, half + j, (mate + na - 2 * j) % na)

    for g in range(nt):
        bsrc[g] = accd[g * tg:(g + 1) * tg].astype(BF16)

    def base_copy(j):
        return tensor_copy(bsrc.at[(t + j) % nt], brecv.at[j], 2, j, (t + j) % nt)

    for j in range(1, nt):
        base_copy(j).start()
    brecv[0] = bsrc[t]

    for j in range(1, na):
        adapter_copy(low2.at[0], low2.at[j], 2, j, (a + j) % na).wait_recv()
    low_all = low2[0].astype(F32)
    for j in range(1, na):
        low_all += low2[j].astype(F32)
    _, _, request_g = tables(tg, t * tg)
    low_all = jnp.where(request_g == iota((tg, LANES), 1) // R, low_all, 0.0).astype(BF16)
    for j in range(1, nt):
        other = (t + nt - j) % nt
        tensor_copy(br_all.at[other], br_all.at[other], 0, j, (t + j) % nt).wait_recv()
    delta = dot(low_all, br_all[...].reshape(nt * rows_t, df)).astype(BF16).astype(F32)

    for j in range(1, nt):
        base_copy(j).wait_recv()
    base = brecv[0].astype(F32)
    for j in range(1, nt):
        base += brecv[j].astype(F32)
    mixed = (base + delta).astype(BF16)

    fq = df // 4
    o_row, o_col = iota((na * 16, tg), 0), iota((na * 16, tg), 1)
    result = jnp.zeros((na * 16, fq), F32)
    for q in range(4):
        hit = ((o_row % 16) // 4 == q) & (o_col == (o_row // 16) * 4 + o_row % 4)
        result += dot(jnp.where(hit, 1.0, 0.0).astype(BF16), mixed[:, q * fq:(q + 1) * fq])
    packed[...] = result.astype(BF16).reshape(na, 16, fq)

    def out_copy(j):
        target = (a + j) % na
        return adapter_copy(packed.at[target], out_ref.at[a], 3, j, target)

    for j in range(1, na):
        out_copy(j).start()
    out_ref[a] = packed[a]
    for j in range(1, na):
        other = (a + na - j) % na
        adapter_copy(packed.at[other], out_ref.at[other], 3, j, other).wait_recv()

    for k in range(len(steps)):
        for c in range(CHUNKS):
            x_copy(k, c).wait_send()
    for j in range(1, na):
        br_copy(j).wait_send()
        adapter_copy(shr.at[0], shr.at[j], 1, j, (a + j) % na).wait_send()
        adapter_copy(low2.at[0], low2.at[j], 2, j, (a + j) % na).wait_send()
        out_copy(j).wait_send()
        for p in range(len(pieces)):
            h_copy(p, j).wait_send()
    for j in range(1, nt):
        tensor_copy(br_all.at[t], br_all.at[t], 0, j, (t + j) % nt).wait_send()
        low_copy(j).wait_send()
        base_copy(j).wait_send()


def local(nt, na, x, w_gate, w_up, w_down, a_gate, a_up, b_gate, b_up, a_down, b_down,
          lengths, request_adapter, placement):
    tok, d_model = x.shape
    tokens = tok * nt * na
    f0 = w_gate.shape[1]
    f = -(-f0 // LANES) * LANES
    df = w_down.shape[1]
    w_down = w_down.reshape(na, f0, df)
    if f != f0:
        wide = ((0, 0), (0, f - f0))
        w_gate, w_up = jnp.pad(w_gate, wide), jnp.pad(w_up, wide)
        b_gate, b_up = jnp.pad(b_gate, wide), jnp.pad(b_up, wide)
        a_down = jnp.pad(a_down, ((0, f - f0), (0, 0)))
        w_down = jnp.pad(w_down, ((0, 0), (0, f - f0), (0, 0)))
    x = x.reshape(tok * 4, d_model // 4)
    b_gate, b_up = b_gate.reshape(-1, R, f), b_up.reshape(-1, R, f)
    starts = [256 * p for p in range(max(f // 256, 1))]
    pieces = tuple(zip(starts, starts[1:] + [f]))
    n = nt * na
    kc = d_model // 4 // CHUNKS
    ranks = a_down.shape[1]
    rows_t = LANES // nt
    tg = tokens // nt
    nsteps = n.bit_length() - 1
    anyspace = pl.BlockSpec(memory_space=pl.ANY)
    smem = pl.BlockSpec(memory_space=pltpu.SMEM)
    dma = pltpu.SemaphoreType.DMA
    out = pl.pallas_call(
        functools.partial(kernel, nt, na, pieces),
        out_shape=jax.ShapeDtypeStruct((na, 16, df // 4), BF16),
        in_specs=[anyspace] * 10 + [smem] * 3,
        out_specs=pl.BlockSpec(memory_space=pltpu.VMEM),
        scratch_shapes=[
            pltpu.VMEM((CHUNKS, n, 16, kc), BF16),
            pltpu.VMEM((2, 4, tokens, kc), BF16),
            pltpu.VMEM((256, 256), BF16),
            pltpu.VMEM((2, tokens, tokens), BF16),
            pltpu.VMEM((2, 4, kc, 2 * f), BF16),
            pltpu.VMEM((na, f, df), BF16),
            pltpu.VMEM((d_model, 2 * LANES), BF16),
            pltpu.VMEM((2, ranks // R, R, f), BF16),
            pltpu.VMEM((2, LANES, f), BF16),
            pltpu.VMEM((f, ranks), BF16),
            pltpu.VMEM((LANES, b_down.shape[1]), BF16),
            pltpu.VMEM((tokens, 2 * f), F32),
            pltpu.VMEM((tokens, 2 * LANES), F32),
            pltpu.VMEM((na, tokens // 4, LANES), BF16),
            pltpu.VMEM((2, tokens, LANES), BF16),
            pltpu.VMEM((na, tokens, f), BF16),
            pltpu.VMEM((tokens, df), F32),
            pltpu.VMEM((na, LANES, df), BF16),
            pltpu.VMEM((na, rows_t, df), BF16),
            pltpu.VMEM((nt, rows_t, df), BF16),
            pltpu.VMEM((nt, tg, LANES), BF16),
            pltpu.VMEM((nt, tg, LANES), BF16),
            pltpu.VMEM((na, tg, LANES), BF16),
            pltpu.VMEM((nt, tg, df), BF16),
            pltpu.VMEM((nt, tg, df), BF16),
            pltpu.VMEM((na, 16, df // 4), BF16),
            dma((2, 4, 2)),
            dma((11,)),
            dma((nsteps, CHUNKS)),
            dma((nsteps, CHUNKS)),
            dma((4, na)),
            dma((4, na)),
            dma((3, nt)),
            dma((3, nt)),
            dma((len(pieces), na)),
            dma((len(pieces), na)),
        ],
        compiler_params=pltpu.CompilerParams(
            collective_id=0, has_side_effects=True, vmem_limit_bytes=60 * 1024 * 1024),
    )(x, w_gate, w_up, w_down, a_gate, a_up, b_gate, b_up, a_down, b_down,
      lengths, request_adapter, placement)
    out = out.reshape(na, 4, tok, df // 4).transpose(2, 0, 1, 3)
    return out.reshape(tok, na * df)


def solution(mesh):
    nt, na = mesh.shape["tensor"], mesh.shape["adapter"]
    both = ("tensor", "adapter")
    in_specs = (
        P(both, None),
        P(None, both),
        P(None, both),
        P("tensor", "adapter"),
        P(None, "adapter"),
        P(None, "adapter"),
        P(None, both),
        P(None, both),
        P(both, None),
        P("adapter", None),
        P(),
        P(),
        P(),
    )
    return jax.shard_map(
        functools.partial(local, nt, na), mesh=mesh, in_specs=in_specs,
        out_specs=P(both, None), check_vma=False)
```

```python
import functools

import jax
import jax.numpy as jnp
from jax import lax
from jax.experimental import pallas as pl
from jax.experimental.pallas import tpu as pltpu
from jax.sharding import PartitionSpec as P

R = 16
LANES = 128
CHUNKS = 4
MESH = pl.DeviceIdType.MESH
F32 = jnp.float32
BF16 = jnp.bfloat16


def dot(a, b):
    return jnp.dot(a, b, preferred_element_type=F32)


def iota(shape, axis):
    return lax.broadcasted_iota(jnp.int32, shape, axis)


def kernel(
    nt, na, pieces, x_ref, wg_ref, wu_ref, wd_ref, ag_ref, au_ref, bg_ref, bu_ref, ad_ref, bd_ref,
    len_ref, radp_ref, plc_ref, out_ref,
    xbuf, xc, split, canon, wbuf, wd, ab, bgu, bsel, ad, bd, acc, acc_s, shr, spread, hbuf, accd,
    breq, br_recv, br_all, low_src, low_recv, low2, bsrc, brecv, packed,
    wsem, lsem, xs_sem, xr_sem, as_sem, ar_sem, ts_sem, tr_sem, hs_sem, hr_sem,
):
    t, a = lax.axis_index("tensor"), lax.axis_index("adapter")
    tokens = acc_s.shape[0]
    f = ad.shape[0]
    d_model = ab.shape[0]
    df = accd.shape[1]
    kc = xc.shape[2] // 4
    kq = d_model // 4
    n = na * nt
    tg = tokens // nt
    rows_t = br_recv.shape[1]
    slots = LANES // R
    reqs = len_ref.shape[0]

    def adapter_copy(src, dst, kind, j, target):
        return pltpu.make_async_remote_copy(
            src_ref=src, dst_ref=dst, send_sem=as_sem.at[kind, j], recv_sem=ar_sem.at[kind, j],
            device_id=(t, target), device_id_type=MESH)

    def tensor_copy(src, dst, kind, j, target):
        return pltpu.make_async_remote_copy(
            src_ref=src, dst_ref=dst, send_sem=ts_sem.at[kind, j], recv_sem=tr_sem.at[kind, j],
            device_id=(target, a), device_id_type=MESH)

    def w_copies(c):
        got = []
        for q in range(4):
            rows = pl.ds(q * kq + c * kc, kc)
            got.append(pltpu.make_async_copy(
                wg_ref.at[rows, :], wbuf.at[c % 2, pl.ds(q * kc, kc), pl.ds(0, f)], wsem.at[c % 2, q, 0]))
            got.append(pltpu.make_async_copy(
                wu_ref.at[rows, :], wbuf.at[c % 2, pl.ds(q * kc, kc), pl.ds(f, f)], wsem.at[c % 2, q, 1]))
        return got

    x_own = [pltpu.make_async_copy(
        x_ref.at[:, pl.ds(c * kc, kc)], xbuf.at[c, 0], lsem.at[c]) for c in range(CHUNKS)]
    load_bd = pltpu.make_async_copy(bd_ref, bd, lsem.at[4])
    load_ag = pltpu.make_async_copy(ag_ref, ab.at[:, pl.ds(0, LANES)], lsem.at[5])
    load_au = pltpu.make_async_copy(au_ref, ab.at[:, pl.ds(LANES, LANES)], lsem.at[6])
    load_bg = pltpu.make_async_copy(bg_ref, bgu.at[0], lsem.at[7])
    load_bu = pltpu.make_async_copy(bu_ref, bgu.at[1], lsem.at[8])
    load_ad = pltpu.make_async_copy(ad_ref, ad, lsem.at[9])
    load_wd = pltpu.make_async_copy(wd_ref, wd, lsem.at[10])
    for copy in x_own + [load_bd] + w_copies(0) + [load_ag, load_au] + w_copies(1):
        copy.start()
    for copy in (load_bg, load_bu, load_ad, load_wd):
        copy.start()

    barrier = pltpu.get_barrier_semaphore()
    for j in range(1, na):
        pl.semaphore_signal(barrier, inc=1, device_id=(t, (a + j) % na), device_id_type=MESH)
    for j in range(1, nt):
        pl.semaphore_signal(barrier, inc=1, device_id=((t + j) % nt, a), device_id_type=MESH)
    pl.semaphore_wait(barrier, na + nt - 2)

    steps = []
    bit = na // 2
    while bit:
        steps.append((0, bit))
        bit //= 2
    bit = nt // 2
    while bit:
        steps.append((1, bit))
        bit //= 2

    def flip(v, b):
        return v + b - 2 * b * ((v // b) % 2)

    def x_copy(k, c):
        axis, b = steps[k]
        target = (t, flip(a, b)) if axis == 0 else (flip(t, b), a)
        return pltpu.make_async_remote_copy(
            src_ref=xbuf.at[c, pl.ds(0, 1 << k)], dst_ref=xbuf.at[c, pl.ds(1 << k, 1 << k)],
            send_sem=xs_sem.at[k, c], recv_sem=xr_sem.at[k, c],
            device_id=target, device_id_type=MESH)

    last = len(steps) - 1

    def x_start(k, c):
        if k == 0:
            x_own[c].wait()
        else:
            x_copy(k - 1, c).wait_recv()
        x_copy(k, c).start()

    for wave in range(CHUNKS + last - 1):
        for k in range(last):
            if 0 <= wave - k < CHUNKS:
                x_start(k, wave - k)

    def tables(rows, first):
        position = iota((rows, LANES), 0) + first
        adapter = jnp.zeros((rows, LANES), jnp.int32)
        slot = jnp.zeros((rows, LANES), jnp.int32)
        request = jnp.zeros((rows, LANES), jnp.int32)
        start = 0
        for r in range(reqs):
            end = start + len_ref[r]
            inside = (position >= start) & (position < end)
            adapter = jnp.where(inside, radp_ref[r], adapter)
            slot = jnp.where(inside, plc_ref[radp_ref[r]], slot)
            request = jnp.where(inside, r, request)
            start = end
        return adapter, slot, request

    row, col = iota((LANES, LANES), 0), iota((LANES, LANES), 1)
    slot_of_row = jnp.full((LANES, LANES), -1, jnp.int32)
    for r in range(reqs):
        slot_of_row = jnp.where(row // R == r, plc_ref[radp_ref[r]], slot_of_row)
    choose = (slot_of_row == a * slots + col // R) & (row % R == col % R)
    choose = jnp.where(choose, 1.0, 0.0).astype(BF16)
    load_bd.wait()

    def choose_block(i, carry):
        off = pl.multiple_of(i * df, LANES)
        breq[i] = dot(choose, bd[:, pl.ds(off, df)]).astype(BF16)
        return carry

    lax.fori_loop(0, na, choose_block, 0)
    own_rows = pl.ds(pl.multiple_of(t * rows_t, rows_t), rows_t)

    def br_copy(j):
        target = (a + j) % na
        return adapter_copy(breq.at[target, own_rows], br_recv.at[j], 0, j, target)

    for j in range(1, na):
        br_copy(j).start()
    br_recv[0] = breq[a, own_rows]

    s_row, s_col = iota((256, 256), 0), iota((256, 256), 1)
    hit = (s_row // 64 == s_col % 4) & (s_row % 64 == s_col // 4)
    split[...] = jnp.where(hit, 1.0, 0.0).astype(BF16)

    def owner_row(place):
        s = place // 4
        src_t, src_a = jnp.full_like(s, t), jnp.full_like(s, a)
        for k, (axis, b) in enumerate(steps):
            on = ((s // (1 << k)) % 2) == 1
            if axis == 0:
                src_a = jnp.where(on, src_a + (b - 2 * b * ((a // b) % 2)), src_a)
            else:
                src_t = jnp.where(on, src_t + (b - 2 * b * ((t // b) % 2)), src_t)
        return (src_t * na + src_a) * 4 + place % 4

    c_row, c_col = iota((tokens, tokens), 0), iota((tokens, tokens), 1)
    canon[0] = jnp.where(c_row == owner_row(c_col), 1.0, 0.0).astype(BF16)
    canon[1] = jnp.where(c_col == owner_row(c_row), 1.0, 0.0).astype(BF16)
    adapter_t, slot_t, request_t = tables(tokens, 0)

    tile = 256
    quarter = tokens // 4

    def arrive(c):
        if c + 1 < CHUNKS:
            x_start(last, c + 1)
        x_copy(last, c).wait_recv()

        def arrange(g, carry):
            block = xbuf[c, pl.ds(g * 16, 16)].reshape(256, kc)
            value = dot(split[...], block).astype(BF16)
            for q in range(4):
                xc[c % 2, pl.ds(pl.multiple_of(g * 64, 64), 64), q * kc:(q + 1) * kc] = value[q * 64:(q + 1) * 64]
            return carry

        lax.fori_loop(0, n // 16, arrange, 0)
        if c == 0:
            load_ag.wait()
            load_au.wait()
        part = dot(xc[c % 2, :, 0:kc], ab[pl.ds(c * kc, kc), :])
        for q in range(1, 4):
            part += dot(xc[c % 2, :, q * kc:(q + 1) * kc], ab[pl.ds(q * kq + c * kc, kc), :])
        if c == 0:
            acc_s[...] = part
        else:
            acc_s[...] += part

    def gate_up(c, i):
        cols = pl.ds(i * tile, tile)
        s = dot(xc[c % 2], wbuf[c % 2, :, cols])
        if c == 0:
            acc[:, cols] = s
        else:
            acc[:, cols] += s

    def whole_chunk(c):
        for copy in w_copies(c):
            copy.wait()

        for i in range(2 * f // tile):
            gate_up(c, i)
        if c + 2 < CHUNKS:
            for copy in w_copies(c + 2):
                copy.start()

    x_start(last, 0)
    for c in range(CHUNKS - 2):
        arrive(c)
        whole_chunk(c)
    arrive(CHUNKS - 2)
    arrive(CHUNKS - 1)

    ordered = dot(canon[0], acc_s[...].astype(BF16))
    total = jnp.zeros((quarter, LANES), F32)
    for h in range(2):
        kept = jnp.where(slot_t == a * slots + iota((tokens, LANES), 1) // R,
                         ordered[:, h * LANES:(h + 1) * LANES], 0.0).astype(BF16)
        for g in range(4):
            to = (col // 32 == g) & ((col % 32) // R == h) & (row % R == col % R)
            total += dot(kept[g * quarter:(g + 1) * quarter],
                         jnp.where(to, 1.0, 0.0).astype(BF16))
    shr[0] = total.astype(BF16)
    for j in range(1, na):
        adapter_copy(shr.at[0], shr.at[j], 1, j, (a + j) % na).start()

    whole_chunk(CHUNKS - 2)

    load_bg.wait()
    load_bu.wait()
    for r in range(reqs):
        for h in range(2):
            bsel[h, r * R:(r + 1) * R] = bgu[h, radp_ref[r]]
    for j in range(1, na):
        adapter_copy(shr.at[0], shr.at[j], 1, j, (a + j) % na).wait_recv()
    shrunk = shr[0].astype(F32)
    for j in range(1, na):
        shrunk += shr[j].astype(F32)
    shrunk = shrunk.astype(BF16)
    for h in range(2):
        parts = []
        for g in range(4):
            frm = (row // 32 == g) & ((row % 32) // R == h) & (row % R == col % R)
            parts.append(dot(shrunk, jnp.where(frm, 1.0, 0.0).astype(BF16)))
        value = jnp.concatenate(parts, axis=0)
        value = jnp.where(request_t == iota((tokens, LANES), 1) // R, value, 0.0).astype(BF16)
        spread[h] = dot(canon[1], value).astype(BF16)

    half = na // 2
    mate = flip(a, 1)

    def h_copy(p, j):
        cols = pl.ds(pieces[p][0], pieces[p][1] - pieces[p][0])
        frm = 0 if j < half else j - half
        target = (a + 2 * j) % na if j < half else mate
        return pltpu.make_async_remote_copy(
            src_ref=hbuf.at[frm, :, cols], dst_ref=hbuf.at[j, :, cols],
            send_sem=hs_sem.at[p, j], recv_sem=hr_sem.at[p, j],
            device_id=(t, target), device_id_type=MESH)

    for copy in w_copies(CHUNKS - 1):
        copy.wait()
    full, odd = f // 256, (f // LANES) % 2
    for p, (lo, hi) in enumerate(pieces):
        tiles = [p] if p < full else []
        if odd and p == 0:
            tiles.append(full)
        if p < full:
            tiles.append(full + odd + p)
        for i in tiles:
            gate_up(CHUNKS - 1, i)
        for c0 in range(lo, hi, LANES):
            gate = acc[:, c0:c0 + LANES] + dot(spread[0], bsel[0, :, c0:c0 + LANES])
            up = acc[:, f + c0:f + c0 + LANES] + dot(spread[1], bsel[1, :, c0:c0 + LANES])
            value = (gate / (1.0 + jnp.exp(-gate)) * up).astype(BF16)
            hbuf[0, :, c0:c0 + LANES] = dot(canon[0], value).astype(BF16)
        h_copy(p, half).start()
        for j in range(1, half):
            h_copy(p, j).start()

    for j in range(1, na):
        br_copy(j).wait_recv()
    rows_sum = br_recv[0].astype(F32)
    for j in range(1, na):
        rows_sum += br_recv[j].astype(F32)
    br_all[t] = rows_sum.astype(BF16)
    for j in range(1, nt):
        tensor_copy(br_all.at[t], br_all.at[t], 0, j, (t + j) % nt).start()

    load_ad.wait()

    low = jnp.zeros((tokens, LANES), F32)
    for i in range(ad.shape[1] // 256):
        value = dot(hbuf[0], ad[:, i * 256:(i + 1) * 256])
        for h in range(2):
            owner = (2 * i + h) * slots + iota((tokens, LANES), 1) // R
            low += jnp.where(adapter_t == owner, value[:, h * LANES:(h + 1) * LANES], 0.0)
    same = jnp.where(row % R == col % R, 1.0, 0.0).astype(BF16)
    low = dot(low.astype(BF16), same).astype(BF16)
    for g in range(nt):
        low_src[g] = low[g * tg:(g + 1) * tg]

    def low_copy(j):
        return tensor_copy(low_src.at[(t + j) % nt], low_recv.at[j], 1, j, (t + j) % nt)

    for j in range(1, nt):
        low_copy(j).start()
    low_recv[0] = low_src[t]
    for j in range(1, nt):
        low_copy(j).wait_recv()
    low_sum = low_recv[0].astype(F32)
    for j in range(1, nt):
        low_sum += low_recv[j].astype(F32)
    low2[0] = low_sum.astype(BF16)
    for j in range(1, na):
        adapter_copy(low2.at[0], low2.at[j], 2, j, (a + j) % na).start()

    load_wd.wait()

    dtile = 512 if df % 512 == 0 else LANES

    def down(p, j, source):
        lo, hi = pieces[p] if p >= 0 else (0, f)
        for c0 in range(0, df, dtile):
            value = dot(hbuf[j, :, lo:hi], wd[source, lo:hi, c0:c0 + dtile])
            if p < 0:
                accd[:, c0:c0 + dtile] = value
            else:
                accd[:, c0:c0 + dtile] += value

    down(-1, 0, a)
    for p in range(len(pieces)):
        for j in range(1, half):
            h_copy(p, j).wait_recv()
            h_copy(p, half + j).start()
        for j in range(1, half):
            down(p, j, (a + na - 2 * j) % na)
        h_copy(p, half).wait_recv()
        down(p, half, mate)
    for p in range(len(pieces)):
        for j in range(1, half):
            h_copy(p, half + j).wait_recv()
            down(p, half + j, (mate + na - 2 * j) % na)

    for g in range(nt):
        bsrc[g] = accd[g * tg:(g + 1) * tg].astype(BF16)

    def base_copy(j):
        return tensor_copy(bsrc.at[(t + j) % nt], brecv.at[j], 2, j, (t + j) % nt)

    for j in range(1, nt):
        base_copy(j).start()
    brecv[0] = bsrc[t]

    for j in range(1, na):
        adapter_copy(low2.at[0], low2.at[j], 2, j, (a + j) % na).wait_recv()
    low_all = low2[0].astype(F32)
    for j in range(1, na):
        low_all += low2[j].astype(F32)
    _, _, request_g = tables(tg, t * tg)
    low_all = jnp.where(request_g == iota((tg, LANES), 1) // R, low_all, 0.0).astype(BF16)
    for j in range(1, nt):
        other = (t + nt - j) % nt
        tensor_copy(br_all.at[other], br_all.at[other], 0, j, (t + j) % nt).wait_recv()
    delta = dot(low_all, br_all[...].reshape(nt * rows_t, df)).astype(BF16).astype(F32)

    for j in range(1, nt):
        base_copy(j).wait_recv()
    base = brecv[0].astype(F32)
    for j in range(1, nt):
        base += brecv[j].astype(F32)
    mixed = (base + delta).astype(BF16)

    fq = df // 4
    o_row, o_col = iota((na * 16, tg), 0), iota((na * 16, tg), 1)
    result = jnp.zeros((na * 16, fq), F32)
    for q in range(4):
        hit = ((o_row % 16) // 4 == q) & (o_col == (o_row // 16) * 4 + o_row % 4)
        result += dot(jnp.where(hit, 1.0, 0.0).astype(BF16), mixed[:, q * fq:(q + 1) * fq])
    packed[...] = result.astype(BF16).reshape(na, 16, fq)

    def out_copy(j):
        target = (a + j) % na
        return adapter_copy(packed.at[target], out_ref.at[a], 3, j, target)

    for j in range(1, na):
        out_copy(j).start()
    out_ref[a] = packed[a]
    for j in range(1, na):
        other = (a + na - j) % na
        adapter_copy(packed.at[other], out_ref.at[other], 3, j, other).wait_recv()

    for k in range(len(steps)):
        for c in range(CHUNKS):
            x_copy(k, c).wait_send()
    for j in range(1, na):
        br_copy(j).wait_send()
        adapter_copy(shr.at[0], shr.at[j], 1, j, (a + j) % na).wait_send()
        adapter_copy(low2.at[0], low2.at[j], 2, j, (a + j) % na).wait_send()
        out_copy(j).wait_send()
        for p in range(len(pieces)):
            h_copy(p, j).wait_send()
    for j in range(1, nt):
        tensor_copy(br_all.at[t], br_all.at[t], 0, j, (t + j) % nt).wait_send()
        low_copy(j).wait_send()
        base_copy(j).wait_send()


def local(nt, na, x, w_gate, w_up, w_down, a_gate, a_up, b_gate, b_up, a_down, b_down,
          lengths, request_adapter, placement):
    tok, d_model = x.shape
    tokens = tok * nt * na
    f0 = w_gate.shape[1]
    f = -(-f0 // LANES) * LANES
    df = w_down.shape[1]
    w_down = w_down.reshape(na, f0, df)
    if f != f0:
        wide = ((0, 0), (0, f - f0))
        w_gate, w_up = jnp.pad(w_gate, wide), jnp.pad(w_up, wide)
        b_gate, b_up = jnp.pad(b_gate, wide), jnp.pad(b_up, wide)
        a_down = jnp.pad(a_down, ((0, f - f0), (0, 0)))
        w_down = jnp.pad(w_down, ((0, 0), (0, f - f0), (0, 0)))
    x = x.reshape(tok * 4, d_model // 4)
    b_gate, b_up = b_gate.reshape(-1, R, f), b_up.reshape(-1, R, f)
    starts = [256 * p for p in range(max(f // 256, 1))]
    pieces = tuple(zip(starts, starts[1:] + [f]))
    n = nt * na
    kc = d_model // 4 // CHUNKS
    ranks = a_down.shape[1]
    rows_t = LANES // nt
    tg = tokens // nt
    nsteps = n.bit_length() - 1
    anyspace = pl.BlockSpec(memory_space=pl.ANY)
    smem = pl.BlockSpec(memory_space=pltpu.SMEM)
    dma = pltpu.SemaphoreType.DMA
    out = pl.pallas_call(
        functools.partial(kernel, nt, na, pieces),
        out_shape=jax.ShapeDtypeStruct((na, 16, df // 4), BF16),
        in_specs=[anyspace] * 10 + [smem] * 3,
        out_specs=pl.BlockSpec(memory_space=pltpu.VMEM),
        scratch_shapes=[
            pltpu.VMEM((CHUNKS, n, 16, kc), BF16),
            pltpu.VMEM((2, tokens, 4 * kc), BF16),
            pltpu.VMEM((256, 256), BF16),
            pltpu.VMEM((2, tokens, tokens), BF16),
            pltpu.VMEM((2, 4 * kc, 2 * f), BF16),
            pltpu.VMEM((na, f, df), BF16),
            pltpu.VMEM((d_model, 2 * LANES), BF16),
            pltpu.VMEM((2, ranks // R, R, f), BF16),
            pltpu.VMEM((2, LANES, f), BF16),
            pltpu.VMEM((f, ranks), BF16),
            pltpu.VMEM((LANES, b_down.shape[1]), BF16),
            pltpu.VMEM((tokens, 2 * f), F32),
            pltpu.VMEM((tokens, 2 * LANES), F32),
            pltpu.VMEM((na, tokens // 4, LANES), BF16),
            pltpu.VMEM((2, tokens, LANES), BF16),
            pltpu.VMEM((na, tokens, f), BF16),
            pltpu.VMEM((tokens, df), F32),
            pltpu.VMEM((na, LANES, df), BF16),
            pltpu.VMEM((na, rows_t, df), BF16),
            pltpu.VMEM((nt, rows_t, df), BF16),
            pltpu.VMEM((nt, tg, LANES), BF16),
            pltpu.VMEM((nt, tg, LANES), BF16),
            pltpu.VMEM((na, tg, LANES), BF16),
            pltpu.VMEM((nt, tg, df), BF16),
            pltpu.VMEM((nt, tg, df), BF16),
            pltpu.VMEM((na, 16, df // 4), BF16),
            dma((2, 4, 2)),
            dma((11,)),
            dma((nsteps, CHUNKS)),
            dma((nsteps, CHUNKS)),
            dma((4, na)),
            dma((4, na)),
            dma((3, nt)),
            dma((3, nt)),
            dma((len(pieces), na)),
            dma((len(pieces), na)),
        ],
        compiler_params=pltpu.CompilerParams(
            collective_id=0, has_side_effects=True, vmem_limit_bytes=60 * 1024 * 1024),
    )(x, w_gate, w_up, w_down, a_gate, a_up, b_gate, b_up, a_down, b_down,
      lengths, request_adapter, placement)
    out = out.reshape(na, 4, tok, df // 4).transpose(2, 0, 1, 3)
    return out.reshape(tok, na * df)


def solution(mesh):
    nt, na = mesh.shape["tensor"], mesh.shape["adapter"]
    both = ("tensor", "adapter")
    in_specs = (
        P(both, None),
        P(None, both),
        P(None, both),
        P("tensor", "adapter"),
        P(None, "adapter"),
        P(None, "adapter"),
        P(None, both),
        P(None, both),
        P(both, None),
        P("adapter", None),
        P(),
        P(),
        P(),
    )
    return jax.shard_map(
        functools.partial(local, nt, na), mesh=mesh, in_specs=in_specs,
        out_specs=P(both, None), check_vma=False)
```

```python
import functools

import jax
import jax.numpy as jnp
from jax import lax
from jax.experimental import pallas as pl
from jax.experimental.pallas import tpu as pltpu
from jax.sharding import PartitionSpec as P

R = 16
LANES = 128
CHUNKS = 4
MESH = pl.DeviceIdType.MESH
F32 = jnp.float32
BF16 = jnp.bfloat16


def dot(a, b):
    return jnp.dot(a, b, preferred_element_type=F32)


def iota(shape, axis):
    return lax.broadcasted_iota(jnp.int32, shape, axis)


def kernel(
    nt, na, pieces, x_ref, wg_ref, wu_ref, wd_ref, ag_ref, au_ref, bg_ref, bu_ref, ad_ref, bd_ref,
    len_ref, radp_ref, plc_ref, out_ref,
    xbuf, xc, split, canon, wbuf, wd, ab, bgu, bsel, ad, bd, acc, acc_s, shr, spread, hbuf, accd,
    breq, br_recv, br_all, low_src, low_recv, low2, bsrc, brecv, packed,
    wsem, lsem, xs_sem, xr_sem, as_sem, ar_sem, ts_sem, tr_sem, hs_sem, hr_sem,
):
    t, a = lax.axis_index("tensor"), lax.axis_index("adapter")
    tokens = acc_s.shape[0]
    f = ad.shape[0]
    d_model = ab.shape[0]
    df = accd.shape[1]
    kc = xc.shape[2] // 4
    kq = d_model // 4
    n = na * nt
    tg = tokens // nt
    rows_t = br_recv.shape[1]
    slots = LANES // R
    reqs = len_ref.shape[0]

    def adapter_copy(src, dst, kind, j, target):
        return pltpu.make_async_remote_copy(
            src_ref=src, dst_ref=dst, send_sem=as_sem.at[kind, j], recv_sem=ar_sem.at[kind, j],
            device_id=(t, target), device_id_type=MESH)

    def tensor_copy(src, dst, kind, j, target):
        return pltpu.make_async_remote_copy(
            src_ref=src, dst_ref=dst, send_sem=ts_sem.at[kind, j], recv_sem=tr_sem.at[kind, j],
            device_id=(target, a), device_id_type=MESH)

    def w_copies(c):
        got = []
        for q in range(4):
            rows = pl.ds(q * kq + c * kc, kc)
            got.append(pltpu.make_async_copy(
                wg_ref.at[rows, :], wbuf.at[c % 2, pl.ds(q * kc, kc), pl.ds(0, f)], wsem.at[c % 2, q, 0]))
            got.append(pltpu.make_async_copy(
                wu_ref.at[rows, :], wbuf.at[c % 2, pl.ds(q * kc, kc), pl.ds(f, f)], wsem.at[c % 2, q, 1]))
        return got

    x_own = [pltpu.make_async_copy(
        x_ref.at[:, pl.ds(c * kc, kc)], xbuf.at[c, 0], lsem.at[c]) for c in range(CHUNKS)]
    load_bd = pltpu.make_async_copy(bd_ref, bd, lsem.at[4])
    load_ag = pltpu.make_async_copy(ag_ref, ab.at[:, pl.ds(0, LANES)], lsem.at[5])
    load_au = pltpu.make_async_copy(au_ref, ab.at[:, pl.ds(LANES, LANES)], lsem.at[6])
    load_bg = pltpu.make_async_copy(bg_ref, bgu.at[0], lsem.at[7])
    load_bu = pltpu.make_async_copy(bu_ref, bgu.at[1], lsem.at[8])
    load_ad = pltpu.make_async_copy(ad_ref, ad, lsem.at[9])
    load_wd = pltpu.make_async_copy(wd_ref, wd, lsem.at[10])
    for copy in x_own + [load_bd] + w_copies(0) + [load_ag, load_au] + w_copies(1):
        copy.start()
    for copy in (load_bg, load_bu, load_ad, load_wd):
        copy.start()

    barrier = pltpu.get_barrier_semaphore()
    for j in range(1, na):
        pl.semaphore_signal(barrier, inc=1, device_id=(t, (a + j) % na), device_id_type=MESH)
    for j in range(1, nt):
        pl.semaphore_signal(barrier, inc=1, device_id=((t + j) % nt, a), device_id_type=MESH)
    pl.semaphore_wait(barrier, na + nt - 2)

    steps = []
    bit = na // 2
    while bit:
        steps.append((0, bit))
        bit //= 2
    bit = nt // 2
    while bit:
        steps.append((1, bit))
        bit //= 2

    def flip(v, b):
        return v + b - 2 * b * ((v // b) % 2)

    def x_copy(k, c):
        axis, b = steps[k]
        target = (t, flip(a, b)) if axis == 0 else (flip(t, b), a)
        return pltpu.make_async_remote_copy(
            src_ref=xbuf.at[c, pl.ds(0, 1 << k)], dst_ref=xbuf.at[c, pl.ds(1 << k, 1 << k)],
            send_sem=xs_sem.at[k, c], recv_sem=xr_sem.at[k, c],
            device_id=target, device_id_type=MESH)

    last = len(steps) - 1

    def x_start(k, c):
        if k == 0:
            x_own[c].wait()
        else:
            x_copy(k - 1, c).wait_recv()
        x_copy(k, c).start()

    for wave in range(CHUNKS + last - 1):
        for k in range(last):
            if 0 <= wave - k < CHUNKS:
                x_start(k, wave - k)

    def tables(rows, first):
        position = iota((rows, LANES), 0) + first
        adapter = jnp.zeros((rows, LANES), jnp.int32)
        slot = jnp.zeros((rows, LANES), jnp.int32)
        request = jnp.zeros((rows, LANES), jnp.int32)
        start = 0
        for r in range(reqs):
            end = start + len_ref[r]
            inside = (position >= start) & (position < end)
            adapter = jnp.where(inside, radp_ref[r], adapter)
            slot = jnp.where(inside, plc_ref[radp_ref[r]], slot)
            request = jnp.where(inside, r, request)
            start = end
        return adapter, slot, request

    row, col = iota((LANES, LANES), 0), iota((LANES, LANES), 1)
    slot_of_row = jnp.full((LANES, LANES), -1, jnp.int32)
    for r in range(reqs):
        slot_of_row = jnp.where(row // R == r, plc_ref[radp_ref[r]], slot_of_row)
    choose = (slot_of_row == a * slots + col // R) & (row % R == col % R)
    choose = jnp.where(choose, 1.0, 0.0).astype(BF16)
    load_bd.wait()

    def choose_block(i, carry):
        off = pl.multiple_of(i * df, LANES)
        breq[i] = dot(choose, bd[:, pl.ds(off, df)]).astype(BF16)
        return carry

    lax.fori_loop(0, na, choose_block, 0)
    own_rows = pl.ds(pl.multiple_of(t * rows_t, rows_t), rows_t)

    def br_copy(j):
        target = (a + j) % na
        return adapter_copy(breq.at[target, own_rows], br_recv.at[j], 0, j, target)

    for j in range(1, na):
        br_copy(j).start()
    br_recv[0] = breq[a, own_rows]

    s_row, s_col = iota((256, 256), 0), iota((256, 256), 1)
    hit = (s_row // 64 == s_col % 4) & (s_row % 64 == s_col // 4)
    split[...] = jnp.where(hit, 1.0, 0.0).astype(BF16)

    def owner_row(place):
        s = place // 4
        src_t, src_a = jnp.full_like(s, t), jnp.full_like(s, a)
        for k, (axis, b) in enumerate(steps):
            on = ((s // (1 << k)) % 2) == 1
            if axis == 0:
                src_a = jnp.where(on, src_a + (b - 2 * b * ((a // b) % 2)), src_a)
            else:
                src_t = jnp.where(on, src_t + (b - 2 * b * ((t // b) % 2)), src_t)
        return (src_t * na + src_a) * 4 + place % 4

    c_row, c_col = iota((tokens, tokens), 0), iota((tokens, tokens), 1)
    canon[0] = jnp.where(c_row == owner_row(c_col), 1.0, 0.0).astype(BF16)
    canon[1] = jnp.where(c_col == owner_row(c_row), 1.0, 0.0).astype(BF16)
    adapter_t, slot_t, request_t = tables(tokens, 0)

    tile = 256
    quarter = tokens // 4

    def arrive(c):
        if c + 1 < CHUNKS:
            x_start(last, c + 1)
        x_copy(last, c).wait_recv()

        for g in range(n // 16):
            block = xbuf[c, g * 16:(g + 1) * 16].reshape(256, kc)
            value = dot(split[...], block).astype(BF16)
            for q in range(4):
                xc[c % 2, g * 64:(g + 1) * 64, q * kc:(q + 1) * kc] = value[q * 64:(q + 1) * 64]
        if c == 0:
            load_ag.wait()
            load_au.wait()
        part = dot(xc[c % 2, :, 0:kc], ab[pl.ds(c * kc, kc), :])
        for q in range(1, 4):
            part += dot(xc[c % 2, :, q * kc:(q + 1) * kc], ab[pl.ds(q * kq + c * kc, kc), :])
        if c == 0:
            acc_s[...] = part
        else:
            acc_s[...] += part

    def gate_up(c, i):
        cols = pl.ds(i * tile, tile)
        s = dot(xc[c % 2], wbuf[c % 2, :, cols])
        if c == 0:
            acc[:, cols] = s
        else:
            acc[:, cols] += s

    def whole_chunk(c):
        for copy in w_copies(c):
            copy.wait()

        for i in range(2 * f // tile):
            gate_up(c, i)
        if c + 2 < CHUNKS:
            for copy in w_copies(c + 2):
                copy.start()

    x_start(last, 0)
    for c in range(CHUNKS - 2):
        arrive(c)
        whole_chunk(c)
    arrive(CHUNKS - 2)
    arrive(CHUNKS - 1)

    ordered = dot(canon[0], acc_s[...].astype(BF16))
    total = jnp.zeros((quarter, LANES), F32)
    for h in range(2):
        kept = jnp.where(slot_t == a * slots + iota((tokens, LANES), 1) // R,
                         ordered[:, h * LANES:(h + 1) * LANES], 0.0).astype(BF16)
        for g in range(4):
            to = (col // 32 == g) & ((col % 32) // R == h) & (row % R == col % R)
            total += dot(kept[g * quarter:(g + 1) * quarter],
                         jnp.where(to, 1.0, 0.0).astype(BF16))
    shr[0] = total.astype(BF16)
    for j in range(1, na):
        adapter_copy(shr.at[0], shr.at[j], 1, j, (a + j) % na).start()

    whole_chunk(CHUNKS - 2)

    half = na // 2
    mate = flip(a, 1)

    def h_copy(p, j):
        cols = pl.ds(pieces[p][0], pieces[p][1] - pieces[p][0])
        frm = 0 if j < half else j - half
        target = (a + 2 * j) % na if j < half else mate
        return pltpu.make_async_remote_copy(
            src_ref=hbuf.at[frm, :, cols], dst_ref=hbuf.at[j, :, cols],
            send_sem=hs_sem.at[p, j], recv_sem=hr_sem.at[p, j],
            device_id=(t, target), device_id_type=MESH)

    def spread_shrunk():
        load_bg.wait()
        load_bu.wait()
        for r in range(reqs):
            for h in range(2):
                bsel[h, r * R:(r + 1) * R] = bgu[h, radp_ref[r]]
        for j in range(1, na):
            adapter_copy(shr.at[0], shr.at[j], 1, j, (a + j) % na).wait_recv()
        shrunk = shr[0].astype(F32)
        for j in range(1, na):
            shrunk += shr[j].astype(F32)
        shrunk = shrunk.astype(BF16)
        for h in range(2):
            parts = []
            for g in range(4):
                frm = (row // 32 == g) & ((row % 32) // R == h) & (row % R == col % R)
                parts.append(dot(shrunk, jnp.where(frm, 1.0, 0.0).astype(BF16)))
            value = jnp.concatenate(parts, axis=0)
            value = jnp.where(request_t == iota((tokens, LANES), 1) // R, value, 0.0).astype(BF16)
            spread[h] = dot(canon[1], value).astype(BF16)

    for copy in w_copies(CHUNKS - 1):
        copy.wait()
    made = set()
    for p, (lo, hi) in enumerate(pieces):
        tiles = {c0 // tile for c0 in range(lo, hi, LANES)}
        tiles |= {(f + c0) // tile for c0 in range(lo, hi, LANES)}
        for i in sorted(tiles - made):
            gate_up(CHUNKS - 1, i)
        made |= tiles
        if p == 0:
            spread_shrunk()
        for c0 in range(lo, hi, LANES):
            gate = acc[:, c0:c0 + LANES] + dot(spread[0], bsel[0, :, c0:c0 + LANES])
            up = acc[:, f + c0:f + c0 + LANES] + dot(spread[1], bsel[1, :, c0:c0 + LANES])
            value = (gate / (1.0 + jnp.exp(-gate)) * up).astype(BF16)
            hbuf[0, :, c0:c0 + LANES] = dot(canon[0], value).astype(BF16)
        h_copy(p, half).start()
        for j in range(1, half):
            h_copy(p, j).start()

    def low_copy(j):
        return tensor_copy(low_src.at[(t + j) % nt], low_recv.at[j], 1, j, (t + j) % nt)

    def low_first():
        load_ad.wait()

        low = jnp.zeros((tokens, LANES), F32)
        for i in range(ad.shape[1] // 256):
            value = dot(hbuf[0], ad[:, i * 256:(i + 1) * 256])
            for h in range(2):
                owner = (2 * i + h) * slots + iota((tokens, LANES), 1) // R
                low += jnp.where(adapter_t == owner, value[:, h * LANES:(h + 1) * LANES], 0.0)
        same = jnp.where(row % R == col % R, 1.0, 0.0).astype(BF16)
        low = dot(low.astype(BF16), same).astype(BF16)
        for g in range(nt):
            low_src[g] = low[g * tg:(g + 1) * tg]

        for j in range(1, nt):
            low_copy(j).start()
        low_recv[0] = low_src[t]

    def low_second():
        for j in range(1, nt):
            low_copy(j).wait_recv()
        low_sum = low_recv[0].astype(F32)
        for j in range(1, nt):
            low_sum += low_recv[j].astype(F32)
        low2[0] = low_sum.astype(BF16)
        for j in range(1, na):
            adapter_copy(low2.at[0], low2.at[j], 2, j, (a + j) % na).start()

    load_wd.wait()

    dtile = 512 if df % 512 == 0 else LANES

    def down(p, j, source):
        lo, hi = pieces[p] if p >= 0 else (0, f)
        for c0 in range(0, df, dtile):
            value = dot(hbuf[j, :, lo:hi], wd[source, lo:hi, c0:c0 + dtile])
            if p < 0:
                accd[:, c0:c0 + dtile] = value
            else:
                accd[:, c0:c0 + dtile] += value

    down(-1, 0, a)
    for j in range(1, na):
        br_copy(j).wait_recv()
    rows_sum = br_recv[0].astype(F32)
    for j in range(1, na):
        rows_sum += br_recv[j].astype(F32)
    br_all[t] = rows_sum.astype(BF16)
    for j in range(1, nt):
        tensor_copy(br_all.at[t], br_all.at[t], 0, j, (t + j) % nt).start()

    for p in range(len(pieces)):
        for j in range(1, half):
            h_copy(p, j).wait_recv()
            h_copy(p, half + j).start()
        if p == 0:
            low_first()
        for j in range(1, half):
            down(p, j, (a + na - 2 * j) % na)
        h_copy(p, half).wait_recv()
        down(p, half, mate)
        if p == 0:
            low_second()
    for p in range(len(pieces)):
        for j in range(1, half):
            h_copy(p, half + j).wait_recv()
            down(p, half + j, (mate + na - 2 * j) % na)

    for g in range(nt):
        bsrc[g] = accd[g * tg:(g + 1) * tg].astype(BF16)

    def base_copy(j):
        return tensor_copy(bsrc.at[(t + j) % nt], brecv.at[j], 2, j, (t + j) % nt)

    for j in range(1, nt):
        base_copy(j).start()
    brecv[0] = bsrc[t]

    for j in range(1, na):
        adapter_copy(low2.at[0], low2.at[j], 2, j, (a + j) % na).wait_recv()
    low_all = low2[0].astype(F32)
    for j in range(1, na):
        low_all += low2[j].astype(F32)
    _, _, request_g = tables(tg, t * tg)
    low_all = jnp.where(request_g == iota((tg, LANES), 1) // R, low_all, 0.0).astype(BF16)
    for j in range(1, nt):
        other = (t + nt - j) % nt
        tensor_copy(br_all.at[other], br_all.at[other], 0, j, (t + j) % nt).wait_recv()
    delta = dot(low_all, br_all[...].reshape(nt * rows_t, df)).astype(BF16).astype(F32)

    for j in range(1, nt):
        base_copy(j).wait_recv()
    base = brecv[0].astype(F32)
    for j in range(1, nt):
        base += brecv[j].astype(F32)
    mixed = (base + delta).astype(BF16)

    fq = df // 4
    o_row, o_col = iota((na * 16, tg), 0), iota((na * 16, tg), 1)
    result = jnp.zeros((na * 16, fq), F32)
    for q in range(4):
        hit = ((o_row % 16) // 4 == q) & (o_col == (o_row // 16) * 4 + o_row % 4)
        result += dot(jnp.where(hit, 1.0, 0.0).astype(BF16), mixed[:, q * fq:(q + 1) * fq])
    packed[...] = result.astype(BF16).reshape(na, 16, fq)

    def out_copy(j):
        target = (a + j) % na
        return adapter_copy(packed.at[target], out_ref.at[a], 3, j, target)

    for j in range(1, na):
        out_copy(j).start()
    out_ref[a] = packed[a]
    for j in range(1, na):
        other = (a + na - j) % na
        adapter_copy(packed.at[other], out_ref.at[other], 3, j, other).wait_recv()

    for k in range(len(steps)):
        for c in range(CHUNKS):
            x_copy(k, c).wait_send()
    for j in range(1, na):
        br_copy(j).wait_send()
        adapter_copy(shr.at[0], shr.at[j], 1, j, (a + j) % na).wait_send()
        adapter_copy(low2.at[0], low2.at[j], 2, j, (a + j) % na).wait_send()
        out_copy(j).wait_send()
        for p in range(len(pieces)):
            h_copy(p, j).wait_send()
    for j in range(1, nt):
        tensor_copy(br_all.at[t], br_all.at[t], 0, j, (t + j) % nt).wait_send()
        low_copy(j).wait_send()
        base_copy(j).wait_send()


def local(nt, na, x, w_gate, w_up, w_down, a_gate, a_up, b_gate, b_up, a_down, b_down,
          lengths, request_adapter, placement):
    tok, d_model = x.shape
    tokens = tok * nt * na
    f0 = w_gate.shape[1]
    f = -(-f0 // LANES) * LANES
    df = w_down.shape[1]
    w_down = w_down.reshape(na, f0, df)
    if f != f0:
        wide = ((0, 0), (0, f - f0))
        w_gate, w_up = jnp.pad(w_gate, wide), jnp.pad(w_up, wide)
        b_gate, b_up = jnp.pad(b_gate, wide), jnp.pad(b_up, wide)
        a_down = jnp.pad(a_down, ((0, f - f0), (0, 0)))
        w_down = jnp.pad(w_down, ((0, 0), (0, f - f0), (0, 0)))
    x = x.reshape(tok * 4, d_model // 4)
    b_gate, b_up = b_gate.reshape(-1, R, f), b_up.reshape(-1, R, f)
    starts = [256 * p for p in range(max(f // 256, 1))]
    pieces = tuple(zip(starts, starts[1:] + [f]))[::-1]
    n = nt * na
    kc = d_model // 4 // CHUNKS
    ranks = a_down.shape[1]
    rows_t = LANES // nt
    tg = tokens // nt
    nsteps = n.bit_length() - 1
    anyspace = pl.BlockSpec(memory_space=pl.ANY)
    smem = pl.BlockSpec(memory_space=pltpu.SMEM)
    dma = pltpu.SemaphoreType.DMA
    out = pl.pallas_call(
        functools.partial(kernel, nt, na, pieces),
        out_shape=jax.ShapeDtypeStruct((na, 16, df // 4), BF16),
        in_specs=[anyspace] * 10 + [smem] * 3,
        out_specs=pl.BlockSpec(memory_space=pltpu.VMEM),
        scratch_shapes=[
            pltpu.VMEM((CHUNKS, n, 16, kc), BF16),
            pltpu.VMEM((2, tokens, 4 * kc), BF16),
            pltpu.VMEM((256, 256), BF16),
            pltpu.VMEM((2, tokens, tokens), BF16),
            pltpu.VMEM((2, 4 * kc, 2 * f), BF16),
            pltpu.VMEM((na, f, df), BF16),
            pltpu.VMEM((d_model, 2 * LANES), BF16),
            pltpu.VMEM((2, ranks // R, R, f), BF16),
            pltpu.VMEM((2, LANES, f), BF16),
            pltpu.VMEM((f, ranks), BF16),
            pltpu.VMEM((LANES, b_down.shape[1]), BF16),
            pltpu.VMEM((tokens, 2 * f), F32),
            pltpu.VMEM((tokens, 2 * LANES), F32),
            pltpu.VMEM((na, tokens // 4, LANES), BF16),
            pltpu.VMEM((2, tokens, LANES), BF16),
            pltpu.VMEM((na, tokens, f), BF16),
            pltpu.VMEM((tokens, df), F32),
            pltpu.VMEM((na, LANES, df), BF16),
            pltpu.VMEM((na, rows_t, df), BF16),
            pltpu.VMEM((nt, rows_t, df), BF16),
            pltpu.VMEM((nt, tg, LANES), BF16),
            pltpu.VMEM((nt, tg, LANES), BF16),
            pltpu.VMEM((na, tg, LANES), BF16),
            pltpu.VMEM((nt, tg, df), BF16),
            pltpu.VMEM((nt, tg, df), BF16),
            pltpu.VMEM((na, 16, df // 4), BF16),
            dma((2, 4, 2)),
            dma((11,)),
            dma((nsteps, CHUNKS)),
            dma((nsteps, CHUNKS)),
            dma((4, na)),
            dma((4, na)),
            dma((3, nt)),
            dma((3, nt)),
            dma((len(pieces), na)),
            dma((len(pieces), na)),
        ],
        compiler_params=pltpu.CompilerParams(
            collective_id=0, has_side_effects=True, vmem_limit_bytes=60 * 1024 * 1024),
    )(x, w_gate, w_up, w_down, a_gate, a_up, b_gate, b_up, a_down, b_down,
      lengths, request_adapter, placement)
    out = out.reshape(na, 4, tok, df // 4).transpose(2, 0, 1, 3)
    return out.reshape(tok, na * df)


def solution(mesh):
    nt, na = mesh.shape["tensor"], mesh.shape["adapter"]
    both = ("tensor", "adapter")
    in_specs = (
        P(both, None),
        P(None, both),
        P(None, both),
        P("tensor", "adapter"),
        P(None, "adapter"),
        P(None, "adapter"),
        P(None, both),
        P(None, both),
        P(both, None),
        P("adapter", None),
        P(),
        P(),
        P(),
    )
    return jax.shard_map(
        functools.partial(local, nt, na), mesh=mesh, in_specs=in_specs,
        out_specs=P(both, None), check_vma=False)
```
